32 devices in a mesh: row: 16 (over z, y, x), col: 2 (over core).
Axes of the slice: x: 2, y: 2, z: 4, core: 2. Of those that a mesh axis runs over, the one named last changes fastest.
Arguments:
- queries: bfloat16 [16384, 1024], P(('row', 'col')), may hold values from -150 to 150
- keys: bfloat16 [16384, 128], P(('col', 'row')), may hold values from -6.1 to 6.1
- values: bfloat16 [16384, 128], P(('col', 'row')), may hold values from -6 to 6
- row_ptr: int32 [129], replicated, may hold values from 0 to 2048, as said below
- col_blocks: int32 [2048], replicated, may hold values from 0 to 127, as said below
- w_out: bfloat16 [1024, 8192], replicated, may hold values from -0.1875 to 0.1875
Outputs:
- projected: bfloat16 [16384, 8192], P(('row', 'col'))
The draws below stay inside these ranges and needn't reach their ends.
Inputs may be any that keep to these rules, and one draw needn't show every extreme that they name: row_ptr[0] is 0 and row_ptr never falls; block-row b lists row_ptr[b+1] - row_ptr[b] blocks, 1 to 31; row_ptr[g * 8] = g * 8 * 16 for every g; in every group of 8 consecutive block-rows some block-row lists exactly 31 blocks. col_blocks[e] lies in key group e mod 2, that is between (e mod 2) * 64 and (e mod 2) * 64 + 63; the blocks listed for one block-row are distinct.
All inputs are finite; a program needn't handle non-finite values.
Results may differ from the reference program's by a relative error of at most 0.0055.
Values may be sent and summed in bfloat16 or wider, within the bound.
A program may use at most 192 MiB of HBM per device.

```python
import jax
import jax.numpy as jnp
from jax import lax

D = 8192
HEADS = 8
HEAD_DIM = 128
BLOCK = 128
RPD = 8
AVG = 16
MOST = 31
NB = 128
SEQ = 16384
NNZ = 2048
ROW_GROUPS = 16
KEY_GROUPS = 2
GROUP_BLOCKS = 64


def pattern(key):
    pattern_key = jax.random.fold_in(key, 7001)
    order_key, length_key, rotate_key = jax.random.split(pattern_key, 3)
    ranking = jax.random.randint(order_key, (ROW_GROUPS, RPD), 0, 1 << 20) * RPD + jnp.arange(RPD, dtype=jnp.int32)[None, :]
    ordering = jnp.argsort(ranking, axis=1, stable=True)
    position = jnp.argsort(ordering, axis=1, stable=True)
    pair_count = RPD // 2
    first_half = jax.random.randint(length_key, (ROW_GROUPS, pair_count), 1, 2 * AVG)
    first_half = jnp.where(jnp.arange(pair_count)[None, :] == 0, MOST, first_half)
    paired = jnp.stack([first_half, 2 * AVG - first_half], axis=2).reshape(ROW_GROUPS, RPD)
    lengths = jnp.take_along_axis(paired, position, axis=1).reshape(NB).astype(jnp.int32)
    row_ptr = jnp.concatenate([jnp.zeros((1,), jnp.int32), jnp.cumsum(lengths).astype(jnp.int32)])
    entry_ids = jnp.arange(NNZ, dtype=jnp.int32)
    owners = jnp.clip(jnp.searchsorted(row_ptr, entry_ids, side='right') - 1, 0, NB - 1).astype(jnp.int32)
    group_ids = entry_ids % KEY_GROUPS
    rotation = jax.random.randint(rotate_key, (NB, KEY_GROUPS), 0, GROUP_BLOCKS)
    offsets = (rotation[owners, group_ids] + entry_ids // KEY_GROUPS) % GROUP_BLOCKS
    col_blocks = (group_ids * GROUP_BLOCKS + offsets).astype(jnp.int32)
    return (row_ptr, col_blocks)


def make_keys(key):
    drawn = jax.random.truncated_normal(jax.random.fold_in(key, 7002), -6.0, 6.0, (SEQ, HEAD_DIM), jnp.float32)
    return drawn


def draw_row_ptr(key, part):
    return pattern(key)[0]


def draw_col_blocks(key, part):
    return pattern(key)[1]


def draw_keys(key, part):
    return make_keys(key).astype(jnp.bfloat16)


def draw_queries(key, part):
    drawn = jax.random.truncated_normal(jax.random.fold_in(key, 7003), -6.0, 6.0, (SEQ, HEADS * HEAD_DIM), jnp.float32)
    return drawn.astype(jnp.bfloat16)


def block_levels(key, dims, cuts, low, high):
    gain, own = 1.0, jax.random.fold_in(key, 6)
    for dim, blocks in cuts:
        draws = jnp.exp(jax.random.uniform(jax.random.fold_in(own, dim), (blocks,), jnp.float32, low / len(cuts), high / len(cuts)))
        gain = gain * jnp.repeat(draws, dims[dim] // blocks).reshape([-1 if axis == dim else 1 for axis in range(len(dims))])
    return gain


def normal_values(rng, shape, deviation, reach, shards=(), kind=jnp.bfloat16):
    array = deviation * jax.random.normal(rng, shape, jnp.float32)
    if shards:
        array = array * block_levels(rng, shape, shards, -0.22, 0.18)
    return jnp.clip(array, -reach, reach).astype(kind)


def setup_inputs(seed: int = 0) -> dict:
    streams_of = jax.random.split(jax.random.key(seed), 7)
    queries = draw_queries(jax.random.fold_in(streams_of[6], 71), 0)
    keys = draw_keys(jax.random.fold_in(streams_of[6], 71), 0)
    values = normal_values(streams_of[2], (SEQ, HEAD_DIM), 1.0, 6.0, ((0, 32),))
    row_ptr = draw_row_ptr(jax.random.fold_in(streams_of[6], 71), 0)
    col_blocks = draw_col_blocks(jax.random.fold_in(streams_of[6], 71), 0)
    w_out = normal_values(streams_of[5], (HEADS * HEAD_DIM, D), (HEADS * HEAD_DIM) ** -0.5, 0.1875)
    return dict(queries=queries, keys=keys, values=values, row_ptr=row_ptr, col_blocks=col_blocks, w_out=w_out)


def entry_terms(query_tile, key_tile, value_tile):
    query_heads = query_tile.reshape(BLOCK, HEADS, HEAD_DIM).astype(jnp.float32)
    key_rows = key_tile.astype(jnp.float32)
    value_rows = value_tile.astype(jnp.float32)
    scores = jnp.einsum("qhd,kd->hqk", query_heads, key_rows) * (HEAD_DIM ** -0.5)
    maxima = jnp.max(scores, axis=2)
    exp_scores = jnp.exp(scores - maxima[:, :, None])
    weight_sums = jnp.sum(exp_scores, axis=2)
    weights = exp_scores.astype(jnp.bfloat16).astype(jnp.float32)
    partial_value = jnp.einsum("hqk,kd->qhd", weights, value_rows)
    return maxima.T, weight_sums.T, partial_value


def reference(queries, keys, values, row_ptr, col_blocks, w_out):
    entry_ids = jnp.arange(NNZ, dtype=jnp.int32)
    owners = (jnp.searchsorted(row_ptr, entry_ids, side="right") - 1).astype(jnp.int32)
    initial = (jnp.full((NB, BLOCK, HEADS), -1e30, jnp.float32),
               jnp.zeros((NB, BLOCK, HEADS), jnp.float32),
               jnp.zeros((NB, BLOCK, HEADS, HEAD_DIM), jnp.float32))

    def absorb(running, entry):
        run_max, run_sum, run_out = running
        row_id, col_id = entry
        query_tile = lax.dynamic_slice_in_dim(queries, (row_id * BLOCK).astype(jnp.int32), BLOCK, 0)
        key_tile = lax.dynamic_slice_in_dim(keys, (col_id * BLOCK).astype(jnp.int32), BLOCK, 0)
        value_tile = lax.dynamic_slice_in_dim(values, (col_id * BLOCK).astype(jnp.int32), BLOCK, 0)
        maxima, weight_sums, partial_value = entry_terms(query_tile, key_tile, value_tile)
        old_max = run_max[row_id]
        new_max = jnp.maximum(old_max, maxima)
        keep_old = jnp.exp(old_max - new_max)
        keep_new = jnp.exp(maxima - new_max)
        new_sum = run_sum[row_id] * keep_old + weight_sums * keep_new
        new_out = run_out[row_id] * keep_old[..., None] + partial_value * keep_new[..., None]
        return (run_max.at[row_id].set(new_max), run_sum.at[row_id].set(new_sum),
                run_out.at[row_id].set(new_out)), None

    final, unused = lax.scan(absorb, initial, (owners, col_blocks))
    attention = (final[2] / final[1][..., None]).astype(jnp.bfloat16).reshape(NB, BLOCK, HEADS * HEAD_DIM)

    def project(tile_rows):
        return jnp.dot(tile_rows, w_out, preferred_element_type=jnp.float32).astype(jnp.bfloat16)

    return lax.map(project, attention).reshape(SEQ, D)
```

```python
import functools
import math

import jax
import jax.numpy as jnp
from jax import lax
from jax.experimental import pallas as pl
from jax.experimental.pallas import tpu as pltpu
from jax.sharding import PartitionSpec as P

HEAD_DIM = 128
BLOCK = 128
ONES = 16
CHUNK = 256
LOW = -1e30
RATE = HEAD_DIM ** (-0.5) * math.log2(math.e)
MESH = pl.DeviceIdType.MESH
VMEM_LIMIT = 50 * 1024 * 1024


def grid_of(chips):
    side = 1
    while 4 * (2 * side) ** 2 <= chips:
        side *= 2
    return chips // (side * side), side, side


def near(here, k, size):
    if size == 2:
        return 1 - here
    below, above = here, size - 1 - here
    room = jnp.minimum(below, above)
    side = jnp.where(above >= below, 1, -1)
    both = (k + 1) // 2 * (1 if k % 2 else -1)
    return here + side * jnp.where(k <= 2 * room, both, k - room)


def gather_kernel(sizes, q_ref, k_ref, v_ref, qo_ref, k_all, vt_all, vt, lsem, qsem, ssem, rsem):
    row, col = lax.axis_index("row"), lax.axis_index("col")
    zs, ys, xs = sizes
    here = (row // (ys * xs), row // xs % ys, row % xs)

    def number(place):
        return (place[0] * ys + place[1]) * xs + place[2]

    def beside(axis, step):
        there = list(here)
        there[axis] = here[axis] + step
        inside = jnp.logical_and(there[axis] >= 0, there[axis] < sizes[axis])
        return number(there), inside

    for block in range(v_ref.shape[0] // BLOCK):
        rows = slice(block * BLOCK, (block + 1) * BLOCK)
        vt[rows, :] = v_ref[rows, :].T

    barrier = pltpu.get_barrier_semaphore()
    greeted = 1
    for axis in range(3):
        for step in (-1, 1):
            there, inside = beside(axis, step)

            @pl.when(inside)
            def _():
                pl.semaphore_signal(barrier, inc=1, device_id=(there, col), device_id_type=MESH)

            greeted = greeted + jnp.where(inside, 1, 0)
    pl.semaphore_signal(barrier, inc=1, device_id=(row, 1 - col), device_id_type=MESH)
    pl.semaphore_wait(barrier, greeted)

    alls = (k_all, vt_all)
    owns = (k_ref, vt)
    orders = ((0, 2, 1), (0, 1, 2))
    sends = []

    def copy(piece, origin, source, slot, there):
        return pltpu.make_async_remote_copy(
            src_ref=source,
            dst_ref=alls[piece].at[origin],
            send_sem=ssem.at[piece, origin, slot],
            recv_sem=rsem.at[piece, origin],
            device_id=(there, col),
            device_id_type=MESH,
        )

    def send(piece, origin, source, axis, step, wanted=None):
        there, inside = beside(axis, step)
        if wanted is not None:
            inside = jnp.logical_and(inside, wanted)
        slot = axis * 2 + (step + 1) // 2

        @pl.when(inside)
        def _():
            copy(piece, origin, source, slot, there).start()

        sends.append((inside, piece, origin, source, slot, there))

    def arrive(piece, level, place):
        origin = number(place)
        landed = alls[piece].at[origin]
        copy(piece, origin, landed, 0, row).wait_recv()
        order = orders[piece]
        axis = order[level]
        if sizes[axis] > 2:
            send(piece, origin, landed, axis, 1, place[axis] < here[axis])
            send(piece, origin, landed, axis, -1, place[axis] > here[axis])
        for later in order[level + 1 :]:
            for step in (-1, 1):
                send(piece, origin, landed, later, step)

    to_other = pltpu.make_async_remote_copy(
        src_ref=q_ref,
        dst_ref=qo_ref,
        send_sem=qsem.at[0],
        recv_sem=qsem.at[1],
        device_id=(row, 1 - col),
        device_id_type=MESH,
    )
    for piece in range(2):
        for axis in orders[piece]:
            for step in (-1, 1):
                send(piece, row, owns[piece], axis, step)
    to_other.start()
    keeps = [
        pltpu.make_async_copy(owns[piece], alls[piece].at[row], lsem.at[piece])
        for piece in range(2)
    ]
    for keep in keeps:
        keep.start()

    def placed(piece, ks):
        place = list(here)
        for axis, k in zip(orders[piece], ks):
            if k:
                place[axis] = near(here[axis], k, sizes[axis])
        return place

    lengths = [[sizes[axis] for axis in order] for order in orders]
    for k in range(zs + 1):
        if 0 < k < zs:
            for piece in range(2):
                arrive(piece, 0, placed(piece, (k, 0, 0)))
        if k:
            for piece in range(2):
                for k2 in range(1, lengths[piece][1]):
                    arrive(piece, 1, placed(piece, (k - 1, k2, 0)))
    for k in range(zs):
        for piece in range(2):
            for k2 in range(lengths[piece][1]):
                for k3 in range(1, lengths[piece][2]):
                    arrive(piece, 2, placed(piece, (k, k2, k3)))
    for keep in keeps:
        keep.wait()
    to_other.wait()
    for inside, piece, origin, source, slot, there in sends:

        @pl.when(inside)
        def _():
            copy(piece, origin, source, slot, there).wait_send()


def gathered(queries, keys, values, chips):
    sizes = grid_of(chips)
    whole = jax.ShapeDtypeStruct((chips,) + keys.shape, keys.dtype)
    anywhere = pl.BlockSpec(memory_space=pl.ANY)
    return pl.pallas_call(
        functools.partial(gather_kernel, sizes),
        out_shape=(jax.ShapeDtypeStruct(queries.shape, queries.dtype), whole, whole),
        in_specs=[anywhere, anywhere, pl.BlockSpec(memory_space=pltpu.VMEM)],
        out_specs=(anywhere, anywhere, anywhere),
        scratch_shapes=[
            pltpu.VMEM(values.shape, values.dtype),
            pltpu.SemaphoreType.DMA((2,)),
            pltpu.SemaphoreType.DMA((2,)),
            pltpu.SemaphoreType.DMA((2, chips, 6)),
            pltpu.SemaphoreType.DMA((2, chips)),
        ],
        compiler_params=pltpu.CompilerParams(collective_id=0, has_side_effects=True),
        name="gather",
    )(queries, keys, values)


def attend_kernel(own, ptr_ref, cols_ref, q_ref, k_ref, vt_ref, out_ref, stat_ref, qt, acc, top):
    row, col = lax.axis_index("row"), lax.axis_index("col")
    rows = q_ref.shape[0] // BLOCK
    width = q_ref.shape[1]
    base = col * (k_ref.shape[0] // BLOCK)
    first_row = (row * 2 + (col if own else 1 - col)) * rows

    def step(key_rows, value_cols):
        depth = value_cols.shape[1]
        value_cols = jnp.concatenate(
            [value_cols, jnp.ones((ONES, depth), value_cols.dtype)], axis=0
        )
        for start in range(0, width, CHUNK):
            part = slice(start, start + CHUNK)
            scores = jnp.dot(key_rows, qt[:, part], preferred_element_type=jnp.float32)
            old = top[:, part]
            new = jnp.maximum(old, jnp.max(scores, axis=0, keepdims=True))
            weights = jnp.exp2((scores - new) * RATE).astype(jnp.bfloat16)
            term = jnp.dot(value_cols, weights, preferred_element_type=jnp.float32)
            acc[:, part] = acc[:, part] * jnp.exp2((old - new) * RATE) + term
            top[:, part] = new

    def block_of(ref, entry):
        return ref[pl.ds(pl.multiple_of((cols_ref[entry] - base) * BLOCK, BLOCK), BLOCK), :]

    def block_row(i, carry):
        tokens = pl.ds(pl.multiple_of(i * BLOCK, BLOCK), BLOCK)
        for start in range(0, width, HEAD_DIM):
            head = slice(start, start + HEAD_DIM)
            qt[:, head] = q_ref[tokens, head].T
        acc[...] = jnp.zeros_like(acc)
        top[...] = jnp.full_like(top, LOW)
        begin, end = ptr_ref[first_row + i], ptr_ref[first_row + i + 1]
        first = begin + (begin + col) % 2
        count = jnp.maximum(end - first + 1, 0) // 2

        def pair(t, inner):
            a = first + 4 * t
            b = a + 2
            step(
                jnp.concatenate([block_of(k_ref, a), block_of(k_ref, b)], axis=0),
                jnp.concatenate([block_of(vt_ref, a), block_of(vt_ref, b)], axis=1),
            )
            return inner

        lax.fori_loop(0, count // 2, pair, 0)

        @pl.when(count % 2 == 1)
        def _():
            last = first + 2 * (count - 1)
            step(block_of(k_ref, last), block_of(vt_ref, last))

        out_ref[i] = acc[:HEAD_DIM, :].astype(out_ref.dtype)
        stat_ref[i] = jnp.concatenate(
            [top[...], acc[HEAD_DIM : HEAD_DIM + 7, :]], axis=0
        )
        return carry

    lax.fori_loop(0, rows, block_row, 0)


def attend(own, row_ptr, col_blocks, queries, keys, values_t):
    rows, width = queries.shape[0] // BLOCK, queries.shape[1]
    in_vmem = pl.BlockSpec(memory_space=pltpu.VMEM)
    in_smem = pl.BlockSpec(memory_space=pltpu.SMEM)
    entries = rows * 8
    return pl.pallas_call(
        functools.partial(attend_kernel, own),
        out_shape=(
            jax.ShapeDtypeStruct((rows, HEAD_DIM, width), jnp.bfloat16),
            jax.ShapeDtypeStruct((rows, 8, width), jnp.float32),
        ),
        in_specs=[in_smem, in_smem, in_vmem, in_vmem, in_vmem],
        out_specs=(in_vmem, in_vmem),
        scratch_shapes=[
            pltpu.VMEM((HEAD_DIM, width), jnp.bfloat16),
            pltpu.VMEM((HEAD_DIM + ONES, width), jnp.float32),
            pltpu.VMEM((1, width), jnp.float32),
        ],
        compiler_params=pltpu.CompilerParams(vmem_limit_bytes=VMEM_LIMIT),
        cost_estimate=pl.CostEstimate(
            flops=entries * 8 * 4 * BLOCK * BLOCK * HEAD_DIM,
            bytes_accessed=4 * keys.size,
            transcendentals=entries * BLOCK * width,
        ),
        name="attend_own" if own else "attend_other",
    )(row_ptr, col_blocks, queries, keys, values_t)


def project_kernel(out_a, stat_a, out_b, stat_b, w_ref, o_ref, attention):
    rows, _, width = out_a.shape

    @pl.when(pl.program_id(0) == 0)
    def _():
        for i in range(rows):
            max_a, max_b = stat_a[i, 0:1, :], stat_b[i, 0:1, :]
            peak = jnp.maximum(max_a, max_b)
            scale_a = jnp.exp2((max_a - peak) * RATE)
            scale_b = jnp.exp2((max_b - peak) * RATE)
            total = stat_a[i, 1:2, :] * scale_a + stat_b[i, 1:2, :] * scale_b
            scale_a, scale_b = scale_a / total, scale_b / total
            for start in range(0, width, HEAD_DIM):
                head = slice(start, start + HEAD_DIM)
                joined = (
                    out_a[i, :, head].astype(jnp.float32) * scale_a[:, head]
                    + out_b[i, :, head].astype(jnp.float32) * scale_b[:, head]
                )
                attention[i * BLOCK : (i + 1) * BLOCK, head] = joined.T.astype(attention.dtype)

    o_ref[...] = jnp.dot(
        attention[...], w_ref[...], preferred_element_type=jnp.float32
    ).astype(o_ref.dtype)


def project(own, other, w_out):
    rows, _, width = own[0].shape
    tokens, columns = rows * BLOCK, w_out.shape[1]
    tile = 1024
    partial = pl.BlockSpec(own[0].shape, lambda j: (0, 0, 0))
    stats = pl.BlockSpec(own[1].shape, lambda j: (0, 0, 0))
    return pl.pallas_call(
        project_kernel,
        out_shape=jax.ShapeDtypeStruct((tokens, columns), jnp.bfloat16),
        grid=(columns // tile,),
        in_specs=[
            partial,
            stats,
            partial,
            stats,
            pl.BlockSpec((width, tile), lambda j: (0, j)),
        ],
        out_specs=pl.BlockSpec((tokens, tile), lambda j: (0, j)),
        scratch_shapes=[pltpu.VMEM((tokens, width), jnp.bfloat16)],
        compiler_params=pltpu.CompilerParams(vmem_limit_bytes=VMEM_LIMIT),
        cost_estimate=pl.CostEstimate(
            flops=2 * tokens * width * columns,
            bytes_accessed=2 * (width * columns + tokens * columns),
            transcendentals=0,
        ),
        name="project",
    )(*own, *other, w_out)


def local(queries, keys, values, row_ptr, col_blocks, w_out):
    chips = lax.axis_size("row")
    other_queries, k_all, vt_all = gathered(queries, keys, values, chips)
    k_all = k_all.reshape(-1, HEAD_DIM)
    vt_all = vt_all.reshape(-1, BLOCK)
    for_other = attend(False, row_ptr, col_blocks, other_queries, k_all, vt_all)
    received = [lax.ppermute(part, "col", [(0, 1), (1, 0)]) for part in for_other]
    own = attend(True, row_ptr, col_blocks, queries, k_all, vt_all)
    return project(own, received, w_out)


def solution(mesh):
    in_specs = (
        P(("row", "col"), None),
        P(("col", "row"), None),
        P(("col", "row"), None),
        P(),
        P(),
        P(),
    )
    out_specs = P(("row", "col"), None)
    return jax.shard_map(local, mesh=mesh, in_specs=in_specs, out_specs=out_specs, check_vma=False)
```

```python
import functools
import math

import jax
import jax.numpy as jnp
from jax import lax
from jax.experimental import pallas as pl
from jax.experimental.pallas import tpu as pltpu
from jax.sharding import PartitionSpec as P

HEAD_DIM = 128
BLOCK = 128
ONES = 16
CHUNK = 256
LOW = -1e30
RATE = HEAD_DIM ** (-0.5) * math.log2(math.e)
MESH = pl.DeviceIdType.MESH
VMEM_LIMIT = 50 * 1024 * 1024


def grid_of(chips):
    side = 1
    while 4 * (2 * side) ** 2 <= chips:
        side *= 2
    return chips // (side * side), side, side


def near(here, k, size):
    if size == 2:
        return 1 - here
    below, above = here, size - 1 - here
    room = jnp.minimum(below, above)
    side = jnp.where(above >= below, 1, -1)
    both = (k + 1) // 2 * (1 if k % 2 else -1)
    return here + side * jnp.where(k <= 2 * room, both, k - room)


def gather_kernel(sizes, q_ref, k_ref, v_ref, qo_ref, k_all, vt_all, vt, lsem, qsem, ssem, rsem):
    row, col = lax.axis_index("row"), lax.axis_index("col")
    zs, ys, xs = sizes
    here = (row // (ys * xs), row // xs % ys, row % xs)

    def number(place):
        return (place[0] * ys + place[1]) * xs + place[2]

    def beside(axis, step):
        there = list(here)
        there[axis] = here[axis] + step
        inside = jnp.logical_and(there[axis] >= 0, there[axis] < sizes[axis])
        return number(there), inside

    for block in range(v_ref.shape[0] // BLOCK):
        rows = slice(block * BLOCK, (block + 1) * BLOCK)
        vt[rows, :] = v_ref[rows, :].T

    barrier = pltpu.get_barrier_semaphore()
    greeted = 1
    for axis in range(3):
        for step in (-1, 1):
            there, inside = beside(axis, step)

            @pl.when(inside)
            def _():
                pl.semaphore_signal(barrier, inc=1, device_id=(there, col), device_id_type=MESH)

            greeted = greeted + jnp.where(inside, 1, 0)
    pl.semaphore_signal(barrier, inc=1, device_id=(row, 1 - col), device_id_type=MESH)
    pl.semaphore_wait(barrier, greeted)

    alls = (k_all, vt_all)
    owns = (k_ref, vt)
    orders = ((0, 2, 1), (0, 1, 2))
    sends = []

    def copy(piece, origin, source, slot, there):
        return pltpu.make_async_remote_copy(
            src_ref=source,
            dst_ref=alls[piece].at[origin],
            send_sem=ssem.at[piece, origin, slot],
            recv_sem=rsem.at[piece, origin],
            device_id=(there, col),
            device_id_type=MESH,
        )

    def send(piece, origin, source, axis, step, wanted=None):
        there, inside = beside(axis, step)
        if wanted is not None:
            inside = jnp.logical_and(inside, wanted)
        slot = axis * 2 + (step + 1) // 2

        @pl.when(inside)
        def _():
            copy(piece, origin, source, slot, there).start()

        sends.append((inside, piece, origin, source, slot, there))

    def arrive(piece, level, place):
        origin = number(place)
        landed = alls[piece].at[origin]
        copy(piece, origin, landed, 0, row).wait_recv()
        order = orders[piece]
        axis = order[level]
        if sizes[axis] > 2:
            send(piece, origin, landed, axis, 1, place[axis] < here[axis])
            send(piece, origin, landed, axis, -1, place[axis] > here[axis])
        for later in order[level + 1 :]:
            for step in (-1, 1):
                send(piece, origin, landed, later, step)

    to_other = pltpu.make_async_remote_copy(
        src_ref=q_ref,
        dst_ref=qo_ref,
        send_sem=qsem.at[0],
        recv_sem=qsem.at[1],
        device_id=(row, 1 - col),
        device_id_type=MESH,
    )
    for piece in range(2):
        for axis in orders[piece]:
            for step in (-1, 1):
                send(piece, row, owns[piece], axis, step)
    to_other.start()
    keeps = [
        pltpu.make_async_copy(owns[piece], alls[piece].at[row], lsem.at[piece])
        for piece in range(2)
    ]
    for keep in keeps:
        keep.start()

    def placed(piece, ks):
        place = list(here)
        for axis, k in zip(orders[piece], ks):
            if k:
                place[axis] = near(here[axis], k, sizes[axis])
        return place

    lengths = [[sizes[axis] for axis in order] for order in orders]
    for k in range(zs + 1):
        if 0 < k < zs:
            for piece in range(2):
                arrive(piece, 0, placed(piece, (k, 0, 0)))
        if k:
            for piece in range(2):
                for k2 in range(1, lengths[piece][1]):
                    arrive(piece, 1, placed(piece, (k - 1, k2, 0)))
    for k in range(zs):
        for piece in range(2):
            for k2 in range(lengths[piece][1]):
                for k3 in range(1, lengths[piece][2]):
                    arrive(piece, 2, placed(piece, (k, k2, k3)))
    for keep in keeps:
        keep.wait()
    to_other.wait()
    for inside, piece, origin, source, slot, there in sends:

        @pl.when(inside)
        def _():
            copy(piece, origin, source, slot, there).wait_send()


def gathered(queries, keys, values, chips):
    sizes = grid_of(chips)
    whole = jax.ShapeDtypeStruct((chips,) + keys.shape, keys.dtype)
    anywhere = pl.BlockSpec(memory_space=pl.ANY)
    return pl.pallas_call(
        functools.partial(gather_kernel, sizes),
        out_shape=(jax.ShapeDtypeStruct(queries.shape, queries.dtype), whole, whole),
        in_specs=[anywhere, anywhere, pl.BlockSpec(memory_space=pltpu.VMEM)],
        out_specs=(anywhere, anywhere, anywhere),
        scratch_shapes=[
            pltpu.VMEM(values.shape, values.dtype),
            pltpu.SemaphoreType.DMA((2,)),
            pltpu.SemaphoreType.DMA((2,)),
            pltpu.SemaphoreType.DMA((2, chips, 6)),
            pltpu.SemaphoreType.DMA((2, chips)),
        ],
        compiler_params=pltpu.CompilerParams(collective_id=0, has_side_effects=True),
        name="gather",
    )(queries, keys, values)


def attend_kernel(
    ptr_ref, cols_ref, other_ref, own_ref, k_ref, vt_ref,
    out_other, stat_other, out_own, stat_own,
    row_of, first_of, second_of, both_of, opens, closes, live_of,
    qt, scores_a, scores_b, acc, top,
):
    row, col = lax.axis_index("row"), lax.axis_index("col")
    half_rows = own_ref.shape[0] // BLOCK
    width = own_ref.shape[1]
    base = col * (k_ref.shape[0] // BLOCK)

    def list_row(i, n):
        half = jnp.where(i < half_rows, 1 - col, col)
        block_row = (row * 2 + half) * half_rows + i % half_rows
        begin, end = ptr_ref[block_row], ptr_ref[block_row + 1]
        first = begin + (begin + col) % 2
        count = jnp.maximum(end - first + 1, 0) // 2
        pairs = (count + 1) // 2

        def put(t, n):
            entry = first + 4 * t
            both = 2 * t + 1 < count
            row_of[n] = i
            first_of[n] = cols_ref[entry] - base
            second_of[n] = cols_ref[jnp.where(both, entry + 2, entry)] - base
            both_of[n] = jnp.where(both, 1.0, 0.0)
            live_of[n] = 1.0
            opens[n] = jnp.where(t == 0, 1, 0)
            closes[n] = jnp.where(t == pairs - 1, 1, 0)
            return n + 1

        return lax.fori_loop(0, pairs, put, n)

    number = lax.fori_loop(0, 2 * half_rows, list_row, 0)
    for more in range(2):
        row_of[number + more] = row_of[number - 1]
        first_of[number + more] = first_of[number - 1]
        second_of[number + more] = second_of[number - 1]
        both_of[number + more] = 0.0
        live_of[number + more] = 0.0
        opens[number + more] = 0
        closes[number + more] = 1

    for out, stat in ((out_other, stat_other), (out_own, stat_own)):
        for i in range(half_rows):
            out[i] = jnp.zeros((HEAD_DIM, width), out.dtype)
            stat[i] = jnp.concatenate(
                [jnp.full((1, width), LOW, jnp.float32), jnp.zeros((7, width), jnp.float32)], axis=0
            )
    for half, ref in enumerate((other_ref, own_ref)):
        for i in range(half_rows):
            for start in range(0, width, HEAD_DIM):
                head = slice(start, start + HEAD_DIM)
                qt[half * half_rows + i, :, head] = ref[i * BLOCK : (i + 1) * BLOCK, head].T
    acc[...] = jnp.zeros_like(acc)
    top[...] = jnp.full_like(top, LOW)

    def block_of(ref, block):
        return ref[pl.ds(pl.multiple_of(block * BLOCK, BLOCK), BLOCK), :]

    def keys_of(p):
        return jnp.concatenate(
            [block_of(k_ref, first_of[p]), block_of(k_ref, second_of[p])], axis=0
        )

    def score(p, keys, part, into):
        into[:, part] = jnp.dot(keys, qt[row_of[p], :, part], preferred_element_type=jnp.float32)

    def values_of(p):
        def one(block, weight):
            ones = jnp.ones((ONES, BLOCK), vt_ref.dtype)
            whole = jnp.concatenate([block_of(vt_ref, block), ones], axis=0)
            return whole * jnp.full(whole.shape, weight, jnp.float32).astype(whole.dtype)

        return jnp.concatenate(
            [one(first_of[p], live_of[p]), one(second_of[p], both_of[p])], axis=1
        )

    parts = [slice(start, start + CHUNK) for start in range(0, width, CHUNK)]

    def step(p, scores_now, scores_next):
        keys_next = keys_of(p + 1)
        values = values_of(p)
        fresh = jnp.full((1, CHUNK), opens[p], jnp.int32) == 1
        for part in parts:
            score(p + 1, keys_next, part, scores_next)
            scores = scores_now[:, part]
            old = jnp.where(fresh, LOW, top[:, part])
            new = jnp.maximum(old, jnp.max(scores, axis=0, keepdims=True))
            weights = jnp.exp2((scores - new) * RATE).astype(jnp.bfloat16)
            term = jnp.dot(values, weights, preferred_element_type=jnp.float32)
            acc[:, part] = acc[:, part] * jnp.exp2((old - new) * RATE) + term
            top[:, part] = new
        i = row_of[p]

        def finish(out, stat, at):
            out[at] = acc[:HEAD_DIM, :].astype(out.dtype)
            stat[at] = jnp.concatenate([top[...], acc[HEAD_DIM : HEAD_DIM + 7, :]], axis=0)

        @pl.when(jnp.logical_and(closes[p] == 1, i < half_rows))
        def _():
            finish(out_other, stat_other, i)

        @pl.when(jnp.logical_and(closes[p] == 1, i >= half_rows))
        def _():
            finish(out_own, stat_own, i - half_rows)

    keys = keys_of(0)
    for part in parts:
        score(0, keys, part, scores_a)

    def two(t, carry):
        step(2 * t, scores_a, scores_b)
        step(2 * t + 1, scores_b, scores_a)
        return carry

    lax.fori_loop(0, (number + 1) // 2, two, 0)


def attend(row_ptr, col_blocks, other, own, keys, values_t, entries):
    rows, width = own.shape[0] // BLOCK, own.shape[1]
    in_vmem = pl.BlockSpec(memory_space=pltpu.VMEM)
    in_smem = pl.BlockSpec(memory_space=pltpu.SMEM)
    listed = (entries + 2 * rows) // 2 + 4
    result = (
        jax.ShapeDtypeStruct((rows, HEAD_DIM, width), jnp.bfloat16),
        jax.ShapeDtypeStruct((rows, 8, width), jnp.float32),
    )
    return pl.pallas_call(
        attend_kernel,
        out_shape=result + result,
        in_specs=[in_smem, in_smem] + [in_vmem] * 4,
        out_specs=(in_vmem,) * 4,
        scratch_shapes=[pltpu.SMEM((listed,), jnp.int32)] * 3
        + [pltpu.SMEM((listed,), jnp.float32)]
        + [pltpu.SMEM((listed,), jnp.int32)] * 2
        + [
            pltpu.SMEM((listed,), jnp.float32),
            pltpu.VMEM((2 * rows, HEAD_DIM, width), jnp.bfloat16),
            pltpu.VMEM((2 * BLOCK, width), jnp.float32),
            pltpu.VMEM((2 * BLOCK, width), jnp.float32),
            pltpu.VMEM((HEAD_DIM + ONES, width), jnp.float32),
            pltpu.VMEM((1, width), jnp.float32),
        ],
        compiler_params=pltpu.CompilerParams(vmem_limit_bytes=VMEM_LIMIT),
        cost_estimate=pl.CostEstimate(
            flops=entries * 4 * BLOCK * width * HEAD_DIM,
            bytes_accessed=4 * keys.size,
            transcendentals=entries * BLOCK * width,
        ),
        name="attend",
    )(row_ptr, col_blocks, other, own, keys, values_t)


def project_kernel(out_a, stat_a, out_b, stat_b, w_ref, o_ref, attention):
    rows, _, width = out_a.shape

    @pl.when(pl.program_id(0) == 0)
    def _():
        for i in range(rows):
            max_a, max_b = stat_a[i, 0:1, :], stat_b[i, 0:1, :]
            peak = jnp.maximum(max_a, max_b)
            scale_a = jnp.exp2((max_a - peak) * RATE)
            scale_b = jnp.exp2((max_b - peak) * RATE)
            total = stat_a[i, 1:2, :] * scale_a + stat_b[i, 1:2, :] * scale_b
            scale_a, scale_b = scale_a / total, scale_b / total
            for start in range(0, width, HEAD_DIM):
                head = slice(start, start + HEAD_DIM)
                joined = (
                    out_a[i, :, head].astype(jnp.float32) * scale_a[:, head]
                    + out_b[i, :, head].astype(jnp.float32) * scale_b[:, head]
                )
                attention[i * BLOCK : (i + 1) * BLOCK, head] = joined.T.astype(attention.dtype)

    o_ref[...] = jnp.dot(
        attention[...], w_ref[...], preferred_element_type=jnp.float32
    ).astype(o_ref.dtype)


def project(own, other, w_out):
    rows, _, width = own[0].shape
    tokens, columns = rows * BLOCK, w_out.shape[1]
    tile = 1024
    partial = pl.BlockSpec(own[0].shape, lambda j: (0, 0, 0))
    stats = pl.BlockSpec(own[1].shape, lambda j: (0, 0, 0))
    return pl.pallas_call(
        project_kernel,
        out_shape=jax.ShapeDtypeStruct((tokens, columns), jnp.bfloat16),
        grid=(columns // tile,),
        in_specs=[
            partial,
            stats,
            partial,
            stats,
            pl.BlockSpec((width, tile), lambda j: (0, j)),
        ],
        out_specs=pl.BlockSpec((tokens, tile), lambda j: (0, j)),
        scratch_shapes=[pltpu.VMEM((tokens, width), jnp.bfloat16)],
        compiler_params=pltpu.CompilerParams(vmem_limit_bytes=VMEM_LIMIT),
        cost_estimate=pl.CostEstimate(
            flops=2 * tokens * width * columns,
            bytes_accessed=2 * (width * columns + tokens * columns),
            transcendentals=0,
        ),
        name="project",
    )(*own, *other, w_out)


def local(queries, keys, values, row_ptr, col_blocks, w_out):
    chips = lax.axis_size("row")
    other_queries, k_all, vt_all = gathered(queries, keys, values, chips)
    k_all = k_all.reshape(-1, HEAD_DIM)
    vt_all = vt_all.reshape(-1, BLOCK)
    entries = col_blocks.shape[0] // (chips * lax.axis_size("col"))
    results = attend(row_ptr, col_blocks, other_queries, queries, k_all, vt_all, entries)
    received = [lax.ppermute(part, "col", [(0, 1), (1, 0)]) for part in results[:2]]
    own = results[2:]
    return project(own, received, w_out)


def solution(mesh):
    in_specs = (
        P(("row", "col"), None),
        P(("col", "row"), None),
        P(("col", "row"), None),
        P(),
        P(),
        P(),
    )
    out_specs = P(("row", "col"), None)
    return jax.shard_map(local, mesh=mesh, in_specs=in_specs, out_specs=out_specs, check_vma=False)
```

```python
import functools
import math

import jax
import jax.numpy as jnp
from jax import lax
from jax.experimental import pallas as pl
from jax.experimental.pallas import tpu as pltpu
from jax.sharding import PartitionSpec as P

HEAD_DIM = 128
BLOCK = 128
ONES = 16
CHUNK = 256
LOW = -1e30
RATE = HEAD_DIM ** (-0.5) * math.log2(math.e)
MESH = pl.DeviceIdType.MESH
VMEM_LIMIT = 50 * 1024 * 1024


def grid_of(chips):
    side = 1
    while 4 * (2 * side) ** 2 <= chips:
        side *= 2
    return chips // (side * side), side, side


def near(here, k, size):
    if size == 2:
        return 1 - here
    below, above = here, size - 1 - here
    room = jnp.minimum(below, above)
    side = jnp.where(above >= below, 1, -1)
    both = (k + 1) // 2 * (1 if k % 2 else -1)
    return here + side * jnp.where(k <= 2 * room, both, k - room)


def pieces_of(blocks):
    quarter = blocks // 4
    orders = ((0, 2), (0, 1), (0, 2, 1), (0, 1, 2))
    return [(piece * quarter, quarter, order) for piece, order in enumerate(orders)]


def place_in(piece, place, sizes):
    z, y, x = place
    if piece == 0:
        return z * sizes[2] + x
    if piece == 1:
        return z * sizes[1] + y
    return (z * sizes[1] + y) * sizes[2] + x


def counts_of(sizes):
    zs, ys, xs = sizes
    return (zs * xs, zs * ys, zs * ys * xs, zs * ys * xs)


def gather_kernel(
    sizes, q_ref, k_ref, v_ref, qo_ref, all_0, all_1, all_2, all_3, mine, lsem, qsem, ssem, rsem
):
    row, col = lax.axis_index("row"), lax.axis_index("col")
    zs, ys, xs = sizes
    here = (row // (ys * xs), row // xs % ys, row % xs)
    pieces = pieces_of(k_ref.shape[0] // BLOCK)

    def number(place):
        return (place[0] * ys + place[1]) * xs + place[2]

    def beside(axis, step):
        there = list(here)
        there[axis] = here[axis] + step
        inside = jnp.logical_and(there[axis] >= 0, there[axis] < sizes[axis])
        return number(there), inside

    for piece, (begin, count, _) in enumerate(pieces):
        for block in range(count):
            rows = slice((begin + block) * BLOCK, (begin + block + 1) * BLOCK)
            at = 2 * block * BLOCK
            mine[piece, at : at + BLOCK, :] = k_ref[rows, :]
            mine[piece, at + BLOCK : at + 2 * BLOCK, :] = v_ref[rows, :].T

    barrier = pltpu.get_barrier_semaphore()
    greeted = 1
    for axis in range(3):
        for step in (-1, 1):
            there, inside = beside(axis, step)

            @pl.when(inside)
            def _():
                pl.semaphore_signal(barrier, inc=1, device_id=(there, col), device_id_type=MESH)

            greeted = greeted + jnp.where(inside, 1, 0)
    pl.semaphore_signal(barrier, inc=1, device_id=(row, 1 - col), device_id_type=MESH)
    pl.semaphore_wait(barrier, greeted)

    alls = (all_0, all_1, all_2, all_3)
    orders = [order for _, _, order in pieces]
    sends = []

    def copy(piece, origin, source, slot, there):
        return pltpu.make_async_remote_copy(
            src_ref=source,
            dst_ref=alls[piece].at[origin],
            send_sem=ssem.at[piece, origin, slot],
            recv_sem=rsem.at[piece, origin],
            device_id=(there, col),
            device_id_type=MESH,
        )

    def send(piece, origin, source, axis, step, wanted=None):
        there, inside = beside(axis, step)
        if wanted is not None:
            inside = jnp.logical_and(inside, wanted)
        slot = axis * 2 + (step + 1) // 2

        @pl.when(inside)
        def _():
            copy(piece, origin, source, slot, there).start()

        sends.append((inside, piece, origin, source, slot, there))

    def arrive(piece, level, place):
        origin = place_in(piece, place, sizes)
        landed = alls[piece].at[origin]
        copy(piece, origin, landed, 0, row).wait_recv()
        order = orders[piece]
        axis = order[level]
        if sizes[axis] > 2:
            send(piece, origin, landed, axis, 1, place[axis] < here[axis])
            send(piece, origin, landed, axis, -1, place[axis] > here[axis])
        for later in order[level + 1 :]:
            for step in (-1, 1):
                send(piece, origin, landed, later, step)

    to_other = pltpu.make_async_remote_copy(
        src_ref=q_ref,
        dst_ref=qo_ref,
        send_sem=qsem.at[0],
        recv_sem=qsem.at[1],
        device_id=(row, 1 - col),
        device_id_type=MESH,
    )
    every = range(len(pieces))
    for piece in every:
        for axis in orders[piece]:
            for step in (-1, 1):
                send(piece, place_in(piece, here, sizes), mine.at[piece], axis, step)
    to_other.start()
    keeps = [
        pltpu.make_async_copy(
            mine.at[piece], alls[piece].at[place_in(piece, here, sizes)], lsem.at[piece]
        )
        for piece in every
    ]
    for keep in keeps:
        keep.start()

    def placed(piece, ks):
        place = list(here)
        for axis, k in zip(orders[piece], ks):
            if k:
                place[axis] = near(here[axis], k, sizes[axis])
        return place

    lengths = [[sizes[axis] for axis in order] for order in orders]
    for k in range(zs + 1):
        if 0 < k < zs:
            for piece in every:
                arrive(piece, 0, placed(piece, (k, 0, 0)))
        if k:
            for piece in every:
                for k2 in range(1, lengths[piece][1]):
                    arrive(piece, 1, placed(piece, (k - 1, k2, 0)))
    for k in range(zs):
        for piece in every:
            if len(orders[piece]) > 2:
                for k2 in range(lengths[piece][1]):
                    for k3 in range(1, lengths[piece][2]):
                        arrive(piece, 2, placed(piece, (k, k2, k3)))
    for keep in keeps:
        keep.wait()
    to_other.wait()
    for inside, piece, origin, source, slot, there in sends:

        @pl.when(inside)
        def _():
            copy(piece, origin, source, slot, there).wait_send()


def gathered(queries, keys, values, sizes):
    counts = counts_of(sizes)
    pieces = len(counts)
    rows = 2 * keys.shape[0] // pieces
    anywhere = pl.BlockSpec(memory_space=pl.ANY)
    in_vmem = pl.BlockSpec(memory_space=pltpu.VMEM)
    return pl.pallas_call(
        functools.partial(gather_kernel, sizes),
        out_shape=(jax.ShapeDtypeStruct(queries.shape, queries.dtype),)
        + tuple(jax.ShapeDtypeStruct((count, rows, HEAD_DIM), keys.dtype) for count in counts),
        in_specs=[anywhere, in_vmem, in_vmem],
        out_specs=(anywhere,) * (1 + pieces),
        scratch_shapes=[
            pltpu.VMEM((pieces, rows, HEAD_DIM), keys.dtype),
            pltpu.SemaphoreType.DMA((pieces,)),
            pltpu.SemaphoreType.DMA((2,)),
            pltpu.SemaphoreType.DMA((pieces, counts[-1], 6)),
            pltpu.SemaphoreType.DMA((pieces, counts[-1])),
        ],
        compiler_params=pltpu.CompilerParams(collective_id=0, has_side_effects=True),
        name="gather",
    )(queries, keys, values)


def shifted(part, sizes, axis):
    zs, ys, xs = sizes
    received = []
    for k in range(1, sizes[axis]):
        pairs = []
        for z in range(zs):
            for y in range(ys):
                for x in range(xs):
                    to = [z, y, x]
                    to[axis] = (to[axis] + k) % sizes[axis]
                    pairs.append(((z * ys + y) * xs + x, (to[0] * ys + to[1]) * xs + to[2]))
        received.append(lax.ppermute(part, "row", pairs))
    return received


def attend_kernel(sizes, late, parts, ptr_ref, cols_ref, *refs):
    blocks_in, refs = refs[:parts], refs[parts:]
    if late:
        states, refs = refs[:4], refs[4:]
    else:
        (other_ref, own_ref), refs = refs[:2], refs[2:]
    if late:
        qt_in, refs = refs[0], refs[1:]
    outs, refs = refs[:4], refs[4:]
    if not late:
        qt_out, refs = refs[0], refs[1:]
    row_of, first_of, second_of, both_of, opens, closes, live_of = refs[:7]
    held, sems, scores_a, scores_b, acc, top = refs[7:]
    qt = qt_in if late else qt_out
    out_other, stat_other, out_own, stat_own = outs

    row, col = lax.axis_index("row"), lax.axis_index("col")
    half_rows, _, width = out_own.shape
    zs, ys, xs = sizes
    shift = xs.bit_length() - 1
    counts = counts_of(sizes)
    quarter = blocks_in[0].shape[1] // (2 * BLOCK)
    shard = 4 * quarter
    base = col * (shard * counts[-1])
    my_y, my_x = (row >> shift) & (ys - 1), row & (xs - 1)

    copies = []
    begin = 0
    for index, ref in enumerate(blocks_in):
        copies.append(
            pltpu.make_async_copy(ref, held.at[pl.ds(begin, ref.shape[0])], sems.at[index])
        )
        begin += ref.shape[0]
    for copy in copies:
        copy.start()

    def locate(block):
        origin, within = lax.div(block, shard), lax.rem(block, shard)
        piece, rest = lax.div(within, quarter), lax.rem(within, quarter)
        x, y, z = origin & (xs - 1), (origin >> shift) & (ys - 1), origin >> (2 * shift)
        is_0, is_1 = piece == 0, piece == 1
        here_0, here_1 = z * xs + x, z * ys + y
        if late:
            back_y, back_x = (my_y - y) & (ys - 1), (my_x - x) & (xs - 1)
            held_here = jnp.logical_or(
                jnp.logical_and(is_0, back_y != 0), jnp.logical_and(is_1, back_x != 0)
            )
            place = jnp.where(
                is_0,
                (back_y - 1) * counts[0] + here_0,
                ((ys - 1) + (back_x - 1)) * counts[0] + here_1,
            )
        else:
            held_here = jnp.logical_or(
                jnp.logical_or(piece >= 2, jnp.logical_and(is_0, y == my_y)),
                jnp.logical_and(is_1, x == my_x),
            )
            place = jnp.where(
                is_0,
                here_0,
                jnp.where(
                    is_1,
                    counts[0] + here_1,
                    counts[0] + counts[1] + (piece - 2) * counts[2] + origin,
                ),
            )
        return held_here, place * quarter + rest

    row_of[0] = 0
    first_of[0] = 0
    second_of[0] = 0

    def list_row(i, n):
        half = jnp.where(i < half_rows, 1 - col, col)
        block_row = (row * 2 + half) * half_rows + i % half_rows
        begin, end = ptr_ref[block_row], ptr_ref[block_row + 1]
        first = begin + (begin + col) % 2
        count = jnp.maximum(end - first + 1, 0) // 2

        def put(t, k):
            kept, place = locate(cols_ref[first + 2 * t] - base)
            odd = k & 1
            at = n + (k >> 1)
            start = jnp.where(odd == 1, first_of[at], jnp.where(kept, place, 0))
            first_of[at] = start
            second_of[at] = jnp.where(kept, place, start)
            both_of[at] = jnp.where(jnp.logical_and(kept, odd == 1), 1.0, 0.0)
            live_of[at] = 1.0
            row_of[at] = i
            opens[at] = jnp.where(k < 2, 1, 0)
            closes[at] = 0
            return k + jnp.where(kept, 1, 0)

        k = lax.fori_loop(0, count, put, 0)
        n = n + ((k + 1) >> 1)

        @pl.when(k > 0)
        def _():
            closes[n - 1] = 1

        return n

    number = lax.fori_loop(0, 2 * half_rows, list_row, 0)
    last = jnp.maximum(number - 1, 0)
    for more in range(2):
        row_of[number + more] = row_of[last]
        first_of[number + more] = first_of[last]
        second_of[number + more] = first_of[last]
        both_of[number + more] = 0.0
        live_of[number + more] = 0.0
        opens[number + more] = 0
        closes[number + more] = 1

    if late:
        for out, state in zip(outs, states):
            for i in range(half_rows):
                out[i] = state[i]
    else:
        for out, stat in ((out_other, stat_other), (out_own, stat_own)):
            for i in range(half_rows):
                out[i] = jnp.zeros((HEAD_DIM, width), out.dtype)
                stat[i] = jnp.concatenate(
                    [jnp.full((1, width), LOW, jnp.float32), jnp.zeros((7, width), jnp.float32)],
                    axis=0,
                )
        for half, ref in enumerate((other_ref, own_ref)):
            for i in range(half_rows):
                for start in range(0, width, HEAD_DIM):
                    head = slice(start, start + HEAD_DIM)
                    qt[half * half_rows + i, :, head] = ref[i * BLOCK : (i + 1) * BLOCK, head].T
    acc[...] = jnp.zeros_like(acc)
    top[...] = jnp.full_like(top, LOW)
    for copy in copies:
        copy.wait()

    def block_of(place, values):
        if quarter == 1:
            return held[place, BLOCK * values : BLOCK * (values + 1), :]
        which, rest = lax.div(place, quarter), lax.rem(place, quarter)
        start = pl.multiple_of((2 * rest + values) * BLOCK, BLOCK)
        return held[which, pl.ds(start, BLOCK), :]

    def keys_of(p):
        return jnp.concatenate(
            [block_of(first_of[p], 0), block_of(second_of[p], 0)], axis=0
        )

    def score(p, keys, part, into):
        into[:, part] = jnp.dot(keys, qt[row_of[p], :, part], preferred_element_type=jnp.float32)

    def values_of(p):
        def one(block, weight):
            ones = jnp.ones((ONES, BLOCK), held.dtype)
            whole = jnp.concatenate([block_of(block, 1), ones], axis=0)
            return whole * jnp.full(whole.shape, weight, jnp.float32).astype(whole.dtype)

        return jnp.concatenate(
            [one(first_of[p], live_of[p]), one(second_of[p], both_of[p])], axis=1
        )

    chunks = [slice(start, start + CHUNK) for start in range(0, width, CHUNK)]

    def step(p, scores_now, scores_next):
        i = row_of[p]
        if late:

            def resume(out, stat, at):
                acc[:HEAD_DIM, :] = out[at].astype(jnp.float32)
                acc[HEAD_DIM:, :] = jnp.broadcast_to(stat[at, 1:2, :], (ONES, width))
                top[...] = stat[at, 0:1, :]

            @pl.when(jnp.logical_and(opens[p] == 1, i < half_rows))
            def _():
                resume(states[0], states[1], i)

            @pl.when(jnp.logical_and(opens[p] == 1, i >= half_rows))
            def _():
                resume(states[2], states[3], i - half_rows)

        keys_next = keys_of(p + 1)
        values = values_of(p)
        fresh = jnp.full((1, CHUNK), opens[p], jnp.int32) == 1
        for part in chunks:
            score(p + 1, keys_next, part, scores_next)
            scores = scores_now[:, part]
            old = top[:, part] if late else jnp.where(fresh, LOW, top[:, part])
            new = jnp.maximum(old, jnp.max(scores, axis=0, keepdims=True))
            weights = jnp.exp2((scores - new) * RATE).astype(jnp.bfloat16)
            term = jnp.dot(values, weights, preferred_element_type=jnp.float32)
            acc[:, part] = acc[:, part] * jnp.exp2((old - new) * RATE) + term
            top[:, part] = new

        def finish(out, stat, at):
            out[at] = acc[:HEAD_DIM, :].astype(out.dtype)
            stat[at] = jnp.concatenate([top[...], acc[HEAD_DIM : HEAD_DIM + 7, :]], axis=0)

        @pl.when(jnp.logical_and(closes[p] == 1, i < half_rows))
        def _():
            finish(out_other, stat_other, i)

        @pl.when(jnp.logical_and(closes[p] == 1, i >= half_rows))
        def _():
            finish(out_own, stat_own, i - half_rows)

    keys = keys_of(0)
    for part in chunks:
        score(0, keys, part, scores_a)

    def two(t, carry):
        step(2 * t, scores_a, scores_b)
        step(2 * t + 1, scores_b, scores_a)
        return carry

    lax.fori_loop(0, (number + 1) // 2, two, 0)


def attend(sizes, late, row_ptr, col_blocks, blocks, others, entries, rows):
    width = others[-1].shape[-1]
    anywhere = pl.BlockSpec(memory_space=pl.ANY)
    in_vmem = pl.BlockSpec(memory_space=pltpu.VMEM)
    in_smem = pl.BlockSpec(memory_space=pltpu.SMEM)
    listed = (entries + 2 * rows) // 2 + 4
    result = (
        jax.ShapeDtypeStruct((rows, HEAD_DIM, width), jnp.bfloat16),
        jax.ShapeDtypeStruct((rows, 8, width), jnp.float32),
    ) * 2
    if not late:
        result += (jax.ShapeDtypeStruct((2 * rows, HEAD_DIM, width), jnp.bfloat16),)
    held = sum(part.shape[0] for part in blocks)
    share = entries // 4 if late else 3 * entries // 4
    return pl.pallas_call(
        functools.partial(attend_kernel, sizes, late, len(blocks)),
        out_shape=result,
        in_specs=[in_smem] * 2 + [anywhere] * len(blocks) + [in_vmem] * len(others),
        out_specs=(in_vmem,) * len(result),
        scratch_shapes=[pltpu.SMEM((listed,), jnp.int32)] * 3
        + [pltpu.SMEM((listed,), jnp.float32)]
        + [pltpu.SMEM((listed,), jnp.int32)] * 2
        + [
            pltpu.SMEM((listed,), jnp.float32),
            pltpu.VMEM((held,) + blocks[0].shape[1:], blocks[0].dtype),
            pltpu.SemaphoreType.DMA((len(blocks),)),
            pltpu.VMEM((2 * BLOCK, width), jnp.float32),
            pltpu.VMEM((2 * BLOCK, width), jnp.float32),
            pltpu.VMEM((HEAD_DIM + ONES, width), jnp.float32),
            pltpu.VMEM((1, width), jnp.float32),
        ],
        compiler_params=pltpu.CompilerParams(vmem_limit_bytes=VMEM_LIMIT),
        cost_estimate=pl.CostEstimate(
            flops=share * 4 * BLOCK * width * HEAD_DIM,
            bytes_accessed=2 * held * blocks[0].shape[1] * HEAD_DIM,
            transcendentals=share * BLOCK * width,
        ),
        name="attend_late" if late else "attend_early",
    )(row_ptr, col_blocks, *blocks, *others)


def project_kernel(out_a, stat_a, out_b, stat_b, w_ref, o_ref, attention):
    rows, _, width = out_a.shape

    @pl.when(pl.program_id(0) == 0)
    def _():
        for i in range(rows):
            max_a, max_b = stat_a[i, 0:1, :], stat_b[i, 0:1, :]
            peak = jnp.maximum(max_a, max_b)
            scale_a = jnp.exp2((max_a - peak) * RATE)
            scale_b = jnp.exp2((max_b - peak) * RATE)
            total = stat_a[i, 1:2, :] * scale_a + stat_b[i, 1:2, :] * scale_b
            scale_a, scale_b = scale_a / total, scale_b / total
            for start in range(0, width, HEAD_DIM):
                head = slice(start, start + HEAD_DIM)
                joined = (
                    out_a[i, :, head].astype(jnp.float32) * scale_a[:, head]
                    + out_b[i, :, head].astype(jnp.float32) * scale_b[:, head]
                )
                attention[i * BLOCK : (i + 1) * BLOCK, head] = joined.T.astype(attention.dtype)

    o_ref[...] = jnp.dot(
        attention[...], w_ref[...], preferred_element_type=jnp.float32
    ).astype(o_ref.dtype)


def project(own, other, w_out):
    rows, _, width = own[0].shape
    tokens, columns = rows * BLOCK, w_out.shape[1]
    tile = 1024
    partial = pl.BlockSpec(own[0].shape, lambda j: (0, 0, 0))
    stats = pl.BlockSpec(own[1].shape, lambda j: (0, 0, 0))
    return pl.pallas_call(
        project_kernel,
        out_shape=jax.ShapeDtypeStruct((tokens, columns), jnp.bfloat16),
        grid=(columns // tile,),
        in_specs=[
            partial,
            stats,
            partial,
            stats,
            pl.BlockSpec((width, tile), lambda j: (0, j)),
        ],
        out_specs=pl.BlockSpec((tokens, tile), lambda j: (0, j)),
        scratch_shapes=[pltpu.VMEM((tokens, width), jnp.bfloat16)],
        compiler_params=pltpu.CompilerParams(vmem_limit_bytes=VMEM_LIMIT),
        cost_estimate=pl.CostEstimate(
            flops=2 * tokens * width * columns,
            bytes_accessed=2 * (width * columns + tokens * columns),
            transcendentals=0,
        ),
        name="project",
    )(*own, *other, w_out)


def local(queries, keys, values, row_ptr, col_blocks, w_out):
    chips = lax.axis_size("row")
    sizes = grid_of(chips)
    rows = queries.shape[0] // BLOCK
    entries = col_blocks.shape[0] // (chips * lax.axis_size("col"))
    other_queries, *parts = gathered(queries, keys, values, sizes)
    late = shifted(parts[0], sizes, 1) + shifted(parts[1], sizes, 2)
    early = attend(
        sizes, False, row_ptr, col_blocks, parts, (other_queries, queries), entries, rows
    )
    results = attend(sizes, True, row_ptr, col_blocks, late, early, entries, rows)
    received = [lax.ppermute(part, "col", [(0, 1), (1, 0)]) for part in results[:2]]
    own = results[2:]
    return project(own, received, w_out)


def solution(mesh):
    in_specs = (
        P(("row", "col"), None),
        P(("col", "row"), None),
        P(("col", "row"), None),
        P(),
        P(),
        P(),
    )
    out_specs = P(("row", "col"), None)
    return jax.shard_map(local, mesh=mesh, in_specs=in_specs, out_specs=out_specs, check_vma=False)
```

```python
import functools
import math

import jax
import jax.numpy as jnp
from jax import lax
from jax.experimental import pallas as pl
from jax.experimental.pallas import tpu as pltpu
from jax.sharding import PartitionSpec as P

HEAD_DIM = 128
BLOCK = 128
ONES = 16
CHUNK = 256
LOW = -1e30
RATE = HEAD_DIM ** (-0.5) * math.log2(math.e)
MESH = pl.DeviceIdType.MESH
VMEM_LIMIT = 60 * 1024 * 1024


def grid_of(chips):
    side = 1
    while 4 * (2 * side) ** 2 <= chips:
        side *= 2
    return chips // (side * side), side, side


def near(here, k, size):
    if size == 2:
        return 1 - here
    below, above = here, size - 1 - here
    room = jnp.minimum(below, above)
    side = jnp.where(above >= below, 1, -1)
    both = (k + 1) // 2 * (1 if k % 2 else -1)
    return here + side * jnp.where(k <= 2 * room, both, k - room)


def attend_kernel(
    sizes, slots, ptr_ref, cols_ref, q_ref, k_ref, v_ref, out_ref,
    q_other, k_all, vt_all, qt, weights, alphas, stats, scores_a, scores_b, acc, top,
    sent, sent_stat, got, got_stat, xsem, ssem, rsem,
):
    row, col = lax.axis_index("row"), lax.axis_index("col")
    zs, ys, xs = sizes
    here = (row // (ys * xs), row // xs % ys, row % xs)
    shard = k_ref.shape[0] // BLOCK
    part_blocks = shard // 2
    half_rows = q_ref.shape[0] // BLOCK
    width = q_ref.shape[1]
    chunks = [slice(start, start + CHUNK) for start in range(0, width, CHUNK)]
    heads = [slice(start, start + HEAD_DIM) for start in range(0, width, HEAD_DIM)]

    def number(place):
        return (place[0] * ys + place[1]) * xs + place[2]

    def beside(axis, step):
        there = list(here)
        there[axis] = here[axis] + step
        inside = jnp.logical_and(there[axis] >= 0, there[axis] < sizes[axis])
        return number(there), inside

    for block in range(shard):
        rows = slice(block * BLOCK, (block + 1) * BLOCK)
        k_all[row * shard + block] = k_ref[rows, :]
        vt_all[row * shard + block] = v_ref[rows, :].T

    barrier = pltpu.get_barrier_semaphore()
    greeted = 1
    for axis in range(3):
        for step in (-1, 1):
            there, inside = beside(axis, step)

            @pl.when(inside)
            def _():
                pl.semaphore_signal(barrier, inc=1, device_id=(there, col), device_id_type=MESH)

            greeted = greeted + jnp.where(inside, 1, 0)
    pl.semaphore_signal(barrier, inc=1, device_id=(row, 1 - col), device_id_type=MESH)
    pl.semaphore_wait(barrier, greeted)

    orders = ((0, 2, 1), (0, 1, 2)) * 2
    key_pieces, value_pieces = (0, 1), (2, 3)
    sends = []

    def copy(piece, origin, slot, there):
        held = (k_all if piece < 2 else vt_all).at[
            pl.ds(origin * shard + piece % 2 * part_blocks, part_blocks)
        ]
        return pltpu.make_async_remote_copy(
            src_ref=held,
            dst_ref=held,
            send_sem=ssem.at[piece, origin, slot],
            recv_sem=rsem.at[piece, origin],
            device_id=(there, col),
            device_id_type=MESH,
        )

    def send(piece, origin, axis, step, wanted=None):
        there, inside = beside(axis, step)
        if wanted is not None:
            inside = jnp.logical_and(inside, wanted)
        slot = axis * 2 + (step + 1) // 2

        @pl.when(inside)
        def _():
            copy(piece, origin, slot, there).start()

        sends.append((inside, piece, origin, slot, there))

    def placed(piece, ks):
        place = list(here)
        for axis, k in zip(orders[piece], ks):
            if k:
                place[axis] = near(here[axis], k, sizes[axis])
        return place

    def arrive(piece, level, ks):
        place = placed(piece, ks)
        origin = number(place)
        copy(piece, origin, 0, row).wait_recv()
        order = orders[piece]
        axis = order[level]
        if sizes[axis] > 2:
            send(piece, origin, axis, 1, place[axis] < here[axis])
            send(piece, origin, axis, -1, place[axis] > here[axis])
        for later in order[level + 1 :]:
            for step in (-1, 1):
                send(piece, origin, later, step)

    def lines(pieces, k):
        for piece in pieces:
            arrive(piece, 0, (k, 0, 0))

    def planes(pieces, k):
        for piece in pieces:
            for k2 in range(1, sizes[orders[piece][1]]):
                arrive(piece, 1, (k, k2, 0))

    def ends(pieces):
        for k in range(zs):
            for piece in pieces:
                for k2 in range(sizes[orders[piece][1]]):
                    for k3 in range(1, sizes[orders[piece][2]]):
                        arrive(piece, 2, (k, k2, k3))

    def swap(source, target, index):
        return pltpu.make_async_remote_copy(
            src_ref=source,
            dst_ref=target,
            send_sem=xsem.at[2 * index],
            recv_sem=xsem.at[2 * index + 1],
            device_id=(row, 1 - col),
            device_id_type=MESH,
        )

    for piece in key_pieces:
        for axis in orders[piece]:
            for step in (-1, 1):
                send(piece, row, axis, step)
    to_other = swap(q_ref, q_other, 0)
    to_other.start()

    def turn(ref, begin):
        for i in range(half_rows):
            for head in heads:
                qt[begin + i, :, head] = ref[i * BLOCK : (i + 1) * BLOCK, head].T

    turn(q_ref, half_rows)
    acc[...] = jnp.zeros_like(acc)
    top[...] = jnp.full_like(top, LOW)

    planes(key_pieces, 0)
    for k in range(1, zs):
        lines(key_pieces, k)
        if k < zs - 1:
            planes(key_pieces, k)
    for piece in value_pieces:
        for step in (-1, 1):
            send(piece, row, 0, step)
    if zs > 1:
        planes(key_pieces, zs - 1)
    for piece in value_pieces:
        for axis in orders[piece][1:]:
            for step in (-1, 1):
                send(piece, row, axis, step)
    to_other.wait()
    turn(q_other, 0)

    base = col * k_all.shape[0]
    firsts, counts, starts, pairs = [], [], [], []
    listed = 0
    for i in range(2 * half_rows):
        half = 1 - col if i < half_rows else col
        block_row = (row * 2 + half) * half_rows + i % half_rows
        begin, end = ptr_ref[block_row], ptr_ref[block_row + 1]
        first = begin + ((begin + col) & 1)
        count = jnp.maximum(end - first + 1, 0) >> 1
        firsts.append(first)
        counts.append(count)
        pairs.append((count + 1) >> 1)
        starts.append(listed)
        listed = listed + pairs[-1]

    def block_at(entry):
        block = cols_ref[jnp.clip(entry, 0, cols_ref.shape[0] - 1)] - base
        return jnp.clip(block, 0, k_all.shape[0] - 1)

    def slot_of(p):
        live = p < listed
        at = jnp.clip(p, 0, jnp.maximum(listed - 1, 0))
        i, first, count, start = 0, firsts[0], counts[0], starts[0]
        for j in range(1, 2 * half_rows):
            reached = at >= starts[j]
            i = jnp.where(reached, j, i)
            first = jnp.where(reached, firsts[j], first)
            count = jnp.where(reached, counts[j], count)
            start = jnp.where(reached, starts[j], start)
        t = at - start
        both = 2 * t + 1 < count
        entry = first + 4 * t
        a = block_at(entry)
        b = block_at(jnp.where(both, entry + 2, entry))
        live_a = jnp.where(live, 1.0, 0.0)
        live_b = jnp.where(jnp.logical_and(live, both), 1.0, 0.0)
        opened = jnp.where(jnp.logical_and(live, t == 0), 1, 0)
        return i, a, b, live_a, live_b, opened

    def score(slot, part, into):
        i, a, b = slot[:3]
        keys = jnp.concatenate([k_all[a], k_all[b]], axis=0)
        into[:, part] = jnp.dot(keys, qt[i, :, part], preferred_element_type=jnp.float32)

    def soften(p, scores_now, scores_next):
        following = slot_of(p + 1)
        fresh = jnp.full((1, CHUNK), slot_of(p)[5], jnp.int32) == 1
        for part in chunks:
            score(following, part, scores_next)
            scores = scores_now[:, part]
            old = jnp.where(fresh, LOW, top[:, part])
            new = jnp.maximum(old, jnp.max(scores, axis=0, keepdims=True))
            weights[p, :, part] = jnp.exp2((scores - new) * RATE).astype(weights.dtype)
            alphas[p, :, part] = jnp.exp2((old - new) * RATE)
            stats[p, 0:1, part] = new
            top[:, part] = new

    lines(value_pieces, 1) if zs > 1 else None
    ends(key_pieces)
    opening = slot_of(0)
    for part in chunks:
        score(opening, part, scores_a)

    duties = [functools.partial(planes, value_pieces, 0)]
    for k in range(2, zs):
        duties.append(functools.partial(lines, value_pieces, k))
        duties.append(functools.partial(planes, value_pieces, k - 1))
    if zs > 1:
        duties.append(functools.partial(planes, value_pieces, zs - 1))

    for index, duty in enumerate(duties):
        begin = min(2 * index, slots // 2)
        end = min(begin + 2, slots // 2) if index < len(duties) - 1 else slots // 2
        duty()

        def two(t, carry):
            soften(2 * t, scores_a, scores_b)
            soften(2 * t + 1, scores_b, scores_a)
            return carry

        lax.fori_loop(begin, end, two, 0)

    ends(value_pieces)

    def add(p, carry):
        _, a, b, live_a, live_b, _ = slot_of(p)

        def one(block, live):
            ones = jnp.ones((ONES, BLOCK), vt_all.dtype)
            whole = jnp.concatenate([vt_all[block], ones], axis=0)
            return whole * jnp.full(whole.shape, live, jnp.float32).astype(whole.dtype)

        values = jnp.concatenate([one(a, live_a), one(b, live_b)], axis=1)
        for part in chunks:
            term = jnp.dot(values, weights[p, :, part], preferred_element_type=jnp.float32)
            total = acc[:, part] * alphas[p, :, part] + term
            acc[:, part] = total
            weights[p, :HEAD_DIM, part] = total[:HEAD_DIM].astype(weights.dtype)
            stats[p, 1:2, part] = total[HEAD_DIM : HEAD_DIM + 1]
        return carry

    lax.fori_loop(0, slots, add, 0)

    def row_state(i):
        some = jnp.full((1, width), pairs[i], jnp.int32) > 0
        at = jnp.clip(starts[i] + pairs[i] - 1, 0, slots - 1)
        peak = jnp.where(some, stats[at, 0:1, :], LOW)
        total = jnp.where(some, stats[at, 1:2, :], 0.0)
        return peak, total, weights[at, :HEAD_DIM, :]

    for i in range(half_rows):
        peak, total, summed = row_state(i)
        sent[i] = summed
        sent_stat[i] = jnp.concatenate(
            [peak, total, jnp.zeros((6, width), jnp.float32)], axis=0
        )
    swaps = [swap(sent, got, 1), swap(sent_stat, got_stat, 2)]
    for moving in swaps:
        moving.start()
    for inside, piece, origin, slot, there in sends:

        @pl.when(inside)
        def _():
            copy(piece, origin, slot, there).wait_send()

    for moving in swaps:
        moving.wait()
    for i in range(half_rows):
        max_a, sum_a, out_a = row_state(half_rows + i)
        max_b, sum_b = got_stat[i, 0:1, :], got_stat[i, 1:2, :]
        peak = jnp.maximum(max_a, max_b)
        scale_a = jnp.where(sum_a > 0.0, jnp.exp2((max_a - peak) * RATE), 0.0)
        scale_b = jnp.where(sum_b > 0.0, jnp.exp2((max_b - peak) * RATE), 0.0)
        total = sum_a * scale_a + sum_b * scale_b
        scale_a, scale_b = scale_a / total, scale_b / total
        for head in heads:
            joined = (
                out_a[:, head].astype(jnp.float32) * scale_a[:, head]
                + got[i, :, head].astype(jnp.float32) * scale_b[:, head]
            )
            out_ref[i * BLOCK : (i + 1) * BLOCK, head] = joined.T.astype(out_ref.dtype)


def attend(sizes, entries, row_ptr, col_blocks, queries, keys, values):
    chips = sizes[0] * sizes[1] * sizes[2]
    rows, width = queries.shape[0] // BLOCK, queries.shape[1]
    slots = (entries + 2 * rows) // 2
    slots += slots % 2
    blocks = chips * keys.shape[0] // BLOCK
    in_vmem = pl.BlockSpec(memory_space=pltpu.VMEM)
    in_smem = pl.BlockSpec(memory_space=pltpu.SMEM)
    bf16, f32 = jnp.bfloat16, jnp.float32
    return pl.pallas_call(
        functools.partial(attend_kernel, sizes, slots),
        out_shape=jax.ShapeDtypeStruct(queries.shape, queries.dtype),
        in_specs=[in_smem] * 2 + [in_vmem] * 3,
        out_specs=in_vmem,
        scratch_shapes=[
            pltpu.VMEM(queries.shape, bf16),
            pltpu.VMEM((blocks, BLOCK, HEAD_DIM), bf16),
            pltpu.VMEM((blocks, HEAD_DIM, BLOCK), bf16),
            pltpu.VMEM((2 * rows, HEAD_DIM, width), bf16),
            pltpu.VMEM((slots, 2 * BLOCK, width), bf16),
            pltpu.VMEM((slots, 1, width), f32),
            pltpu.VMEM((slots, 8, width), f32),
            pltpu.VMEM((2 * BLOCK, width), f32),
            pltpu.VMEM((2 * BLOCK, width), f32),
            pltpu.VMEM((HEAD_DIM + ONES, width), f32),
            pltpu.VMEM((1, width), f32),
            pltpu.VMEM((rows, HEAD_DIM, width), bf16),
            pltpu.VMEM((rows, 8, width), f32),
            pltpu.VMEM((rows, HEAD_DIM, width), bf16),
            pltpu.VMEM((rows, 8, width), f32),
            pltpu.SemaphoreType.DMA((6,)),
            pltpu.SemaphoreType.DMA((4, chips, 6)),
            pltpu.SemaphoreType.DMA((4, chips)),
        ],
        compiler_params=pltpu.CompilerParams(
            collective_id=0, has_side_effects=True, vmem_limit_bytes=VMEM_LIMIT
        ),
        name="attend",
    )(row_ptr, col_blocks, queries, keys, values)


def project_kernel(attention, w_ref, o_ref):
    o_ref[...] = jnp.dot(
        attention[...], w_ref[...], preferred_element_type=jnp.float32
    ).astype(o_ref.dtype)


def project(attention, w_out):
    tokens, width = attention.shape
    columns = w_out.shape[1]
    tile = 1024
    return pl.pallas_call(
        project_kernel,
        out_shape=jax.ShapeDtypeStruct((tokens, columns), jnp.bfloat16),
        grid=(columns // tile,),
        in_specs=[
            pl.BlockSpec((tokens, width), lambda j: (0, 0)),
            pl.BlockSpec((width, tile), lambda j: (0, j)),
        ],
        out_specs=pl.BlockSpec((tokens, tile), lambda j: (0, j)),
        compiler_params=pltpu.CompilerParams(vmem_limit_bytes=VMEM_LIMIT),
        cost_estimate=pl.CostEstimate(
            flops=2 * tokens * width * columns,
            bytes_accessed=2 * (width * columns + tokens * columns),
            transcendentals=0,
        ),
        name="project",
    )(attention, w_out)


def local(queries, keys, values, row_ptr, col_blocks, w_out):
    chips = lax.axis_size("row")
    entries = col_blocks.shape[0] // (chips * lax.axis_size("col"))
    attention = attend(
        grid_of(chips), entries, row_ptr, col_blocks, queries, keys, values
    )
    return project(attention, w_out)


def solution(mesh):
    in_specs = (
        P(("row", "col"), None),
        P(("col", "row"), None),
        P(("col", "row"), None),
        P(),
        P(),
        P(),
    )
    out_specs = P(("row", "col"), None)
    return jax.shard_map(local, mesh=mesh, in_specs=in_specs, out_specs=out_specs, check_vma=False)
```

```python
import functools
import math

import jax
import jax.numpy as jnp
from jax import lax
from jax.experimental import pallas as pl
from jax.experimental.pallas import tpu as pltpu
from jax.sharding import PartitionSpec as P

HEAD_DIM = 128
BLOCK = 128
ONES = 16
CHUNK = 256
LOW = -1e30
RATE = HEAD_DIM ** (-0.5) * math.log2(math.e)
MESH = pl.DeviceIdType.MESH
VMEM_LIMIT = 60 * 1024 * 1024
SLOW = 30


def grid_of(chips):
    side = 1
    while 4 * (2 * side) ** 2 <= chips:
        side *= 2
    return chips // (side * side), side, side


def near(here, k, size):
    if size == 2:
        return 1 - here
    below, above = here, size - 1 - here
    room = jnp.minimum(below, above)
    side = jnp.where(above >= below, 1, -1)
    both = (k + 1) // 2 * (1 if k % 2 else -1)
    return here + side * jnp.where(k <= 2 * room, both, k - room)


def attend_kernel(
    sizes, slots, ptr_ref, cols_ref, q_ref, k_ref, v_ref, out_ref,
    q_other, k_all, vt_all, qt, weights, alphas, stats, scores_a, scores_b, acc, top,
    sent, sent_stat, got, got_stat, xsem, ssem, rsem,
):
    row, col = lax.axis_index("row"), lax.axis_index("col")
    zs, ys, xs = sizes
    here = (row // (ys * xs), row // xs % ys, row % xs)
    shard = k_ref.shape[0] // BLOCK
    part_blocks = shard // 2
    half_rows = q_ref.shape[0] // BLOCK
    width = q_ref.shape[1]
    chunks = [slice(start, start + CHUNK) for start in range(0, width, CHUNK)]
    heads = [slice(start, start + HEAD_DIM) for start in range(0, width, HEAD_DIM)]

    def number(place):
        return (place[0] * ys + place[1]) * xs + place[2]

    def beside(axis, step):
        there = list(here)
        there[axis] = here[axis] + step
        inside = jnp.logical_and(there[axis] >= 0, there[axis] < sizes[axis])
        return number(there), inside

    for block in range(shard):
        rows = slice(block * BLOCK, (block + 1) * BLOCK)
        k_all[row * shard + block] = k_ref[rows, :]
        vt_all[row * shard + block] = v_ref[rows, :].T

    barrier = pltpu.get_barrier_semaphore()
    greeted = 1
    for axis in range(3):
        for step in (-1, 1):
            there, inside = beside(axis, step)

            @pl.when(inside)
            def _():
                pl.semaphore_signal(barrier, inc=1, device_id=(there, col), device_id_type=MESH)

            greeted = greeted + jnp.where(inside, 1, 0)
    pl.semaphore_signal(barrier, inc=1, device_id=(row, 1 - col), device_id_type=MESH)
    pl.semaphore_wait(barrier, greeted)

    orders = ((0, 2, 1), (0, 1, 2)) * 2
    key_pieces, value_pieces = (0, 1), (2, 3)
    sends = []

    def copy(piece, origin, slot, there):
        held = (k_all if piece < 2 else vt_all).at[
            pl.ds(origin * shard + piece % 2 * part_blocks, part_blocks)
        ]
        return pltpu.make_async_remote_copy(
            src_ref=held,
            dst_ref=held,
            send_sem=ssem.at[piece, origin, slot],
            recv_sem=rsem.at[piece, origin],
            device_id=(there, col),
            device_id_type=MESH,
        )

    def send(piece, origin, axis, step, wanted=None):
        there, inside = beside(axis, step)
        if wanted is not None:
            inside = jnp.logical_and(inside, wanted)
        slot = axis * 2 + (step + 1) // 2

        @pl.when(inside)
        def _():
            copy(piece, origin, slot, there).start()

        sends.append((inside, piece, origin, slot, there))

    def placed(piece, ks):
        place = list(here)
        for axis, k in zip(orders[piece], ks):
            if k:
                place[axis] = near(here[axis], k, sizes[axis])
        return place

    def arrive(piece, level, ks):
        place = placed(piece, ks)
        origin = number(place)
        copy(piece, origin, 0, row).wait_recv()
        order = orders[piece]
        axis = order[level]
        if sizes[axis] > 2:
            send(piece, origin, axis, 1, place[axis] < here[axis])
            send(piece, origin, axis, -1, place[axis] > here[axis])
        for later in order[level + 1 :]:
            for step in (-1, 1):
                send(piece, origin, later, step)

    def lines(pieces, k):
        for piece in pieces:
            arrive(piece, 0, (k, 0, 0))

    def planes(pieces, k):
        for piece in pieces:
            for k2 in range(1, sizes[orders[piece][1]]):
                arrive(piece, 1, (k, k2, 0))

    def ends(pieces):
        for k in range(zs):
            for piece in pieces:
                for k2 in range(sizes[orders[piece][1]]):
                    for k3 in range(1, sizes[orders[piece][2]]):
                        arrive(piece, 2, (k, k2, k3))

    def swap(source, target, index):
        return pltpu.make_async_remote_copy(
            src_ref=source,
            dst_ref=target,
            send_sem=xsem.at[2 * index],
            recv_sem=xsem.at[2 * index + 1],
            device_id=(row, 1 - col),
            device_id_type=MESH,
        )

    for piece in key_pieces:
        for axis in orders[piece]:
            for step in (-1, 1):
                send(piece, row, axis, step)
    to_other = swap(q_ref, q_other, 0)
    to_other.start()

    def turn(ref, begin):
        for i in range(half_rows):
            for head in heads:
                qt[begin + i, :, head] = ref[i * BLOCK : (i + 1) * BLOCK, head].T

    turn(q_ref, half_rows)
    acc[...] = jnp.zeros_like(acc)
    top[...] = jnp.full_like(top, LOW)

    planes(key_pieces, 0)
    for k in range(1, zs):
        lines(key_pieces, k)
        if k < zs - 1:
            planes(key_pieces, k)
    for piece in value_pieces:
        for step in (-1, 1):
            send(piece, row, 0, step)
    for piece in value_pieces:
        for axis in orders[piece][1:]:
            for step in (-1, 1):
                send(piece, row, axis, step)
    if zs > 1:
        planes(key_pieces, zs - 1)
    to_other.wait()
    turn(q_other, 0)

    base = col * k_all.shape[0]
    firsts, counts, starts, pairs = [], [], [], []
    listed = 0
    for i in range(2 * half_rows):
        half = 1 - col if i < half_rows else col
        block_row = (row * 2 + half) * half_rows + i % half_rows
        begin, end = ptr_ref[block_row], ptr_ref[block_row + 1]
        first = begin + ((begin + col) & 1)
        count = jnp.maximum(end - first + 1, 0) >> 1
        firsts.append(first)
        counts.append(count)
        pairs.append((count + 1) >> 1)
        starts.append(listed)
        listed = listed + pairs[-1]

    def block_at(entry):
        block = cols_ref[jnp.clip(entry, 0, cols_ref.shape[0] - 1)] - base
        return jnp.clip(block, 0, k_all.shape[0] - 1)

    def slot_of(p):
        live = p < listed
        at = jnp.clip(p, 0, jnp.maximum(listed - 1, 0))
        i, first, count, start = 0, firsts[0], counts[0], starts[0]
        for j in range(1, 2 * half_rows):
            reached = at >= starts[j]
            i = jnp.where(reached, j, i)
            first = jnp.where(reached, firsts[j], first)
            count = jnp.where(reached, counts[j], count)
            start = jnp.where(reached, starts[j], start)
        t = at - start
        both = 2 * t + 1 < count
        entry = first + 4 * t
        a = block_at(entry)
        b = block_at(jnp.where(both, entry + 2, entry))
        live_a = jnp.where(live, 1.0, 0.0)
        live_b = jnp.where(jnp.logical_and(live, both), 1.0, 0.0)
        opened = jnp.where(jnp.logical_and(live, t == 0), 1, 0)
        return i, a, b, live_a, live_b, opened

    def score(slot, part, into):
        i, a, b = slot[:3]
        keys = jnp.concatenate([k_all[a], k_all[b]], axis=0)
        into[:, part] = jnp.dot(keys, qt[i, :, part], preferred_element_type=jnp.float32)

    def soften(p, scores_now, scores_next):
        following = slot_of(p + 1)
        fresh = jnp.full((1, CHUNK), slot_of(p)[5], jnp.int32) == 1
        for part in chunks:
            score(following, part, scores_next)
            scores = scores_now[:, part]
            old = jnp.where(fresh, LOW, top[:, part])
            new = jnp.maximum(old, jnp.max(scores, axis=0, keepdims=True))
            weights[p, :, part] = jnp.exp2((scores - new) * RATE).astype(weights.dtype)
            alphas[p, :, part] = jnp.exp2((old - new) * RATE)
            stats[p, 0:1, part] = new
            top[:, part] = new

    if zs > 1:
        lines(value_pieces, 1)
    planes(value_pieces, 0)
    ends(key_pieces)
    opening = slot_of(0)
    for part in chunks:
        score(opening, part, scores_a)

    duties = []
    for k in range(2, zs):
        duties.append((3 * (k - 2), functools.partial(lines, value_pieces, k)))
        duties.append((3 * (k - 2) + 1, functools.partial(planes, value_pieces, k - 1)))
    if zs > 1:
        duties.append((3 * (zs - 2), functools.partial(planes, value_pieces, zs - 1)))
    turns = [min(turn, slots // 2) for turn, _ in duties] + [slots // 2]

    for (_, duty), begin, end in zip(duties, turns, turns[1:]):
        duty()

        def two(t, carry):
            soften(2 * t, scores_a, scores_b)
            soften(2 * t + 1, scores_b, scores_a)
            return carry

        lax.fori_loop(begin, end, two, 0)

    ends(value_pieces)

    def add(p, carry):
        _, a, b, live_a, live_b, _ = slot_of(p)

        def one(block, live):
            ones = jnp.ones((ONES, BLOCK), vt_all.dtype)
            whole = jnp.concatenate([vt_all[block], ones], axis=0)
            return whole * jnp.full(whole.shape, live, jnp.float32).astype(whole.dtype)

        values = jnp.concatenate([one(a, live_a), one(b, live_b)], axis=1)
        for part in chunks:
            term = jnp.dot(values, weights[p, :, part], preferred_element_type=jnp.float32)
            total = acc[:, part] * alphas[p, :, part] + term
            acc[:, part] = total
            weights[p, :HEAD_DIM, part] = total[:HEAD_DIM].astype(weights.dtype)
            stats[p, 1:2, part] = total[HEAD_DIM : HEAD_DIM + 1]
        return carry

    lax.fori_loop(0, slots, add, 0)

    def row_state(i):
        some = jnp.full((1, width), pairs[i], jnp.int32) > 0
        at = jnp.clip(starts[i] + pairs[i] - 1, 0, slots - 1)
        peak = jnp.where(some, stats[at, 0:1, :], LOW)
        total = jnp.where(some, stats[at, 1:2, :], 0.0)
        return peak, total, weights[at, :HEAD_DIM, :]

    for i in range(half_rows):
        peak, total, summed = row_state(i)
        sent[i] = summed
        sent_stat[i] = jnp.concatenate(
            [peak, total, jnp.zeros((6, width), jnp.float32)], axis=0
        )
    swaps = [swap(sent, got, 1), swap(sent_stat, got_stat, 2)]
    for moving in swaps:
        moving.start()
    for inside, piece, origin, slot, there in sends:

        @pl.when(inside)
        def _():
            copy(piece, origin, slot, there).wait_send()

    for moving in swaps:
        moving.wait()
    for i in range(half_rows):
        max_a, sum_a, out_a = row_state(half_rows + i)
        max_b, sum_b = got_stat[i, 0:1, :], got_stat[i, 1:2, :]
        peak = jnp.maximum(max_a, max_b)
        scale_a = jnp.where(sum_a > 0.0, jnp.exp2((max_a - peak) * RATE), 0.0)
        scale_b = jnp.where(sum_b > 0.0, jnp.exp2((max_b - peak) * RATE), 0.0)
        total = sum_a * scale_a + sum_b * scale_b
        scale_a, scale_b = scale_a / total, scale_b / total
        for head in heads:
            joined = (
                out_a[:, head].astype(jnp.float32) * scale_a[:, head]
                + got[i, :, head].astype(jnp.float32) * scale_b[:, head]
            )
            out_ref[i * BLOCK : (i + 1) * BLOCK, head] = joined.T.astype(out_ref.dtype)


def attend(sizes, entries, row_ptr, col_blocks, queries, keys, values):
    chips = sizes[0] * sizes[1] * sizes[2]
    rows, width = queries.shape[0] // BLOCK, queries.shape[1]
    slots = (entries + 2 * rows) // 2
    slots += slots % 2
    blocks = chips * keys.shape[0] // BLOCK
    in_vmem = pl.BlockSpec(memory_space=pltpu.VMEM)
    in_smem = pl.BlockSpec(memory_space=pltpu.SMEM)
    bf16, f32 = jnp.bfloat16, jnp.float32
    buffers = [
        (queries.shape, bf16),
        ((blocks, BLOCK, HEAD_DIM), bf16),
        ((blocks, HEAD_DIM, BLOCK), bf16),
        ((2 * rows, HEAD_DIM, width), bf16),
        ((slots, 2 * BLOCK, width), bf16),
        ((slots, 1, width), f32),
        ((slots, 8, width), f32),
        ((2 * BLOCK, width), f32),
        ((2 * BLOCK, width), f32),
        ((HEAD_DIM + ONES, width), f32),
        ((1, width), f32),
        ((rows, HEAD_DIM, width), bf16),
        ((rows, 8, width), f32),
        ((rows, HEAD_DIM, width), bf16),
        ((rows, 8, width), f32),
    ]
    return pl.pallas_call(
        functools.partial(attend_kernel, sizes, slots),
        out_shape=jax.ShapeDtypeStruct(queries.shape, queries.dtype),
        in_specs=[in_smem] * 2 + [in_vmem] * 3,
        out_specs=in_vmem,
        scratch_shapes=[pltpu.VMEM(shape, kind) for shape, kind in buffers]
        + [
            pltpu.SemaphoreType.DMA((6,)),
            pltpu.SemaphoreType.DMA((4, chips, 6)),
            pltpu.SemaphoreType.DMA((4, chips)),
        ],
        compiler_params=pltpu.CompilerParams(
            collective_id=0, has_side_effects=True, vmem_limit_bytes=VMEM_LIMIT
        ),
        cost_estimate=pl.CostEstimate(
            flops=entries * 4 * BLOCK * width * HEAD_DIM,
            bytes_accessed=SLOW * 4 * blocks * BLOCK * HEAD_DIM,
            transcendentals=entries * BLOCK * width,
        ),
        name="attend",
    )(row_ptr, col_blocks, queries, keys, values)


def project_kernel(attention, w_ref, o_ref):
    o_ref[...] = jnp.dot(
        attention[...], w_ref[...], preferred_element_type=jnp.float32
    ).astype(o_ref.dtype)


def project(attention, w_out):
    tokens, width = attention.shape
    columns = w_out.shape[1]
    tile = 1024
    return pl.pallas_call(
        project_kernel,
        out_shape=jax.ShapeDtypeStruct((tokens, columns), jnp.bfloat16),
        grid=(columns // tile,),
        in_specs=[
            pl.BlockSpec((tokens, width), lambda j: (0, 0)),
            pl.BlockSpec((width, tile), lambda j: (0, j)),
        ],
        out_specs=pl.BlockSpec((tokens, tile), lambda j: (0, j)),
        compiler_params=pltpu.CompilerParams(vmem_limit_bytes=VMEM_LIMIT),
        cost_estimate=pl.CostEstimate(
            flops=2 * tokens * width * columns,
            bytes_accessed=2 * (width * columns + tokens * columns),
            transcendentals=0,
        ),
        name="project",
    )(attention, w_out)


def local(queries, keys, values, row_ptr, col_blocks, w_out):
    chips = lax.axis_size("row")
    entries = col_blocks.shape[0] // (chips * lax.axis_size("col"))
    attention = attend(
        grid_of(chips), entries, row_ptr, col_blocks, queries, keys, values
    )
    return project(attention, w_out)


def solution(mesh):
    in_specs = (
        P(("row", "col"), None),
        P(("col", "row"), None),
        P(("col", "row"), None),
        P(),
        P(),
        P(),
    )
    out_specs = P(("row", "col"), None)
    return jax.shard_map(local, mesh=mesh, in_specs=in_specs, out_specs=out_specs, check_vma=False)
```
